32 devices in a mesh: depth: 4 (over y, x), row: 2 (over core), col: 4 (over z).
Axes of the slice: x: 2, y: 2, z: 4, core: 2. Of those that a mesh axis runs over, the one named last changes fastest.
Arguments:
- tokens: bfloat16 [512, 6144], P(('depth', 'row'), 'col'), may hold values from -6 to 6
- grad_out: bfloat16 [512, 6144], P(('depth', 'row'), 'col'), may hold values from -6 to 6
- w_up: bfloat16 [6144, 24576], P(('col', 'depth'), 'row'), may hold values from -0.078125 to 0.078125
- w_down: bfloat16 [6144, 24576], P(('col', 'depth'), 'row'), may hold values from -0.0390625 to 0.0390625
Outputs:
- grad_in: bfloat16 [512, 6144], P(('depth', 'row'), 'col')
- grad_up: bfloat16 [6144, 24576], P(('col', 'depth'), 'row')
- grad_down: bfloat16 [6144, 24576], P(('col', 'depth'), 'row')
The draws below stay inside these ranges and needn't reach their ends.
All inputs are finite; a program needn't handle non-finite values.
Results may differ from the reference program's by a relative error of at most 0.03.
Values may be sent and summed in bfloat16 or wider, within the bound.
A program may use at most 256 MiB of HBM per device.

```python
import math
import jax
import jax.numpy as jnp
from jax import lax

D = 6144
FF = 24576
TOK_DEV = 128
TOKENS = 512
D_PART = 1536
N_DEPTH = 4
N_COL = 4


def raised(entries, rng, source, target, blocks, factor):
    def block_of(axis_at):
        return (jnp.arange(entries.shape[axis_at]) // (entries.shape[axis_at] // blocks)).reshape((-1,) + (1,) * (entries.ndim - 1 - axis_at))

    one_side = jax.random.permutation(rng, blocks)[block_of(target)]
    far = (block_of(target) + blocks // 2) % blocks
    return jnp.where((block_of(source) == one_side) | (block_of(source) == far), factor * entries, entries)


def levels(stream_key, dims, cuts, least, top_value):
    gain, own = 1.0, jax.random.fold_in(stream_key, 6)
    for dim, shards_of in cuts:
        draws = jnp.exp(jax.random.uniform(jax.random.fold_in(own, dim), (shards_of,), jnp.float32, least / len(cuts), top_value / len(cuts)))
        gain = gain * jnp.repeat(draws, dims[dim] // shards_of).reshape([-1 if axis == dim else 1 for axis in range(len(dims))])
    return gain


def bell_draw(key, dims, width, most, shards=(), kind=jnp.bfloat16):
    values = jax.random.normal(key, dims, jnp.float32) * width
    if len(shards) > 0:
        values = levels(key, dims, shards, -0.22, 0.18) * values
    return jnp.clip(values, min=-most, max=most).astype(kind)


def bell_draw_with(key, dims, spread, bound, split, heavy, held_as=jnp.bfloat16):
    entries = spread * jax.random.normal(key, dims, jnp.float32)
    if split:
        entries = entries * levels(key, dims, split, -0.22, 0.18)
    return jnp.clip(raised(entries, jax.random.fold_in(key, 3), *heavy), -bound, bound).astype(held_as)


def setup_inputs(seed: int = 0) -> dict:
    streams_of = jax.random.split(jax.random.key(seed), 5)
    return {
        "tokens": bell_draw_with(streams_of[0], (TOKENS, D), 1.0, 6.0, ((0, 8), (1, 4)), (0, 1, 8, 2.0)),
        "grad_out": bell_draw(streams_of[1], (TOKENS, D), 1.0, 6.0, ((0, 8), (1, 4))),
        "w_up": bell_draw(streams_of[2], (D, FF), D ** -0.5, 0.078125, ((0, 16), (1, 2))),
        "w_down": bell_draw(streams_of[3], (D, FF), FF ** -0.5, 0.0390625, ((0, 16), (1, 2))),
    }


def gelu_parts(hidden):
    coeff = math.sqrt(2.0 / math.pi)
    cube = hidden * hidden * hidden
    slope_in = jnp.tanh(coeff * (hidden + 0.044715 * cube))
    value = 0.5 * hidden * (1.0 + slope_in)
    slope = 0.5 * (1.0 + slope_in) + 0.5 * hidden * (1.0 - slope_in * slope_in) * coeff * (1.0 + 3.0 * 0.044715 * hidden * hidden)
    return (value, slope)

def block_sum(left, weight):
    left_blocks = jnp.transpose(left.reshape(TOKENS, N_COL, D_PART), (1, 0, 2))
    weight_blocks = weight.reshape(N_COL, D_PART, FF)

    def add_block(carry, pieces):
        part = jnp.dot(pieces[0], pieces[1], preferred_element_type=jnp.float32)
        part = lax.optimization_barrier(part.astype(jnp.bfloat16)).astype(jnp.float32)
        return (carry + part, None)
    total, unused = lax.scan(add_block, jnp.zeros((TOKENS, FF), jnp.float32), (left_blocks, weight_blocks))
    return total

def reference(tokens, grad_out, w_up, w_down):
    hidden_pre = block_sum(tokens, w_up)
    act_value, slope = gelu_parts(hidden_pre)
    act = act_value.astype(jnp.bfloat16)
    act_grad = block_sum(grad_out, w_down)
    hidden_grad = (act_grad * slope).astype(jnp.bfloat16)
    grad_in = jnp.dot(hidden_grad, w_up.T, preferred_element_type=jnp.float32).astype(jnp.bfloat16)
    token_blocks = tokens.reshape(N_DEPTH, TOK_DEV, D)
    grad_blocks = hidden_grad.reshape(N_DEPTH, TOK_DEV, FF)

    def add_quarter(carry, pieces):
        part = jnp.dot(pieces[0].T, pieces[1], preferred_element_type=jnp.float32)
        part = lax.optimization_barrier(part.astype(jnp.bfloat16)).astype(jnp.float32)
        return (carry + part, None)
    grad_up_sum, unused = lax.scan(add_quarter, jnp.zeros((D, FF), jnp.float32), (token_blocks, grad_blocks))
    grad_up = grad_up_sum.astype(jnp.bfloat16)
    grad_down = jnp.dot(grad_out.T, act, preferred_element_type=jnp.float32).astype(jnp.bfloat16)
    return (grad_in, grad_up, grad_down)
```

```python
import math

import jax
import jax.numpy as jnp
from jax import lax
from jax.sharding import PartitionSpec as P


def gelu_parts(hidden):
    coeff = math.sqrt(2.0 / math.pi)
    cube = hidden * hidden * hidden
    slope_in = jnp.tanh(coeff * (hidden + 0.044715 * cube))
    value = 0.5 * hidden * (1.0 + slope_in)
    slope = 0.5 * (1.0 + slope_in) + 0.5 * hidden * (1.0 - slope_in * slope_in) * coeff * (
        1.0 + 3.0 * 0.044715 * hidden * hidden
    )
    return (value, slope)


def line_reduce_scatter(parts, axis, name):
    count = lax.axis_size(name)
    here = lax.axis_index(name)

    def piece(index):
        return lax.dynamic_index_in_dim(
            parts, jnp.clip(index, 0, count - 1), axis, keepdims=False
        )

    up, down = None, None
    for step in range(1, count):
        send_up = piece(here + count - step)
        send_down = piece(here + step - count)
        if up is not None:
            send_up = send_up + up
            send_down = send_down + down
        up = lax.ppermute(send_up, name, [(i, i + 1) for i in range(step)])
        down = lax.ppermute(
            send_down, name, [(i, i - 1) for i in range(count - step, count)]
        )
    own = piece(here).astype(jnp.float32)
    return own + up.astype(jnp.float32) + down.astype(jnp.float32)


def line_all_gather(block, axis, name):
    count = lax.axis_size(name)
    here = lax.axis_index(name)
    ups, downs = [], []
    up = down = block
    for step in range(1, count):
        up = lax.ppermute(up, name, [(i, i + 1) for i in range(step - 1, count - 1)])
        down = lax.ppermute(down, name, [(i, i - 1) for i in range(1, count - step + 1)])
        ups.append(up)
        downs.append(down)
    shape = block.shape[:axis] + (count,) + block.shape[axis:]
    whole = lax.dynamic_update_index_in_dim(
        jnp.zeros(shape, block.dtype), block, here, axis
    )
    for step in range(1, count):
        arrived = jnp.where(here >= step, ups[step - 1], downs[count - step - 1])
        whole = lax.dynamic_update_index_in_dim(
            whole, arrived, lax.rem(here - step + count, count), axis
        )
    return whole


def body(tokens, grad_out, w_up, w_down):
    n_depth, n_row, n_col = (lax.axis_size(a) for a in ("depth", "row", "col"))
    rows, part = tokens.shape
    narrow, hidden = w_up.shape
    group = n_depth * n_row
    total = group * rows
    bunch = total // (n_depth * n_col)
    far = hidden // 4 // 128 * 128
    near = hidden - far
    bf16, f32 = jnp.bfloat16, jnp.float32

    both = jnp.stack([tokens, grad_out]).reshape(2, rows, n_depth, narrow)
    both = jnp.transpose(both, (2, 0, 1, 3))
    both = jnp.broadcast_to(both[:, None], (n_depth, n_row, 2, rows, narrow))
    both = both.reshape(group, 2, rows, narrow)
    both = lax.all_to_all(both, ("depth", "row"), 0, 0, tiled=True)
    x_cols = both[:, 0].reshape(total, narrow)
    dy_cols = both[:, 1].reshape(total, narrow)

    def product(left, right):
        return jnp.dot(left, right, preferred_element_type=f32).astype(bf16)

    def outer(left, right):
        return lax.dot_general(
            left, right, (((0,), (0,)), ((), ())), preferred_element_type=f32
        ).astype(bf16)

    pre_near = product(x_cols, w_up[:, :near])
    pre_near = lax.psum_scatter(pre_near, "depth", scatter_dimension=0, tiled=True)
    far_terms = jnp.concatenate(
        [product(x_cols, w_up[:, near:]), product(dy_cols, w_down[:, near:])], axis=1
    )
    far_terms = line_reduce_scatter(
        far_terms.reshape(n_depth, n_col, bunch, 2 * far), 1, "col"
    ).astype(bf16)
    grad_near = product(dy_cols, w_down[:, :near])
    pre_near, grad_near = lax.optimization_barrier((pre_near, grad_near))
    grad_near = lax.psum_scatter(grad_near, "depth", scatter_dimension=0, tiled=True)
    pre_near = line_reduce_scatter(pre_near.reshape(n_col, bunch, near), 0, "col")
    far_sum = lax.psum_scatter(
        far_terms.reshape(n_depth * bunch, 2 * far), "depth", scatter_dimension=0, tiled=True
    ).astype(f32)
    grad_near = line_reduce_scatter(grad_near.reshape(n_col, bunch, near), 0, "col")

    far_value, far_slope = gelu_parts(far_sum[:, :far])
    far_pair = jnp.concatenate(
        [far_value.astype(bf16), (far_sum[:, far:] * far_slope).astype(bf16)], axis=1
    )
    near_value, near_slope = gelu_parts(pre_near)
    act_near = near_value.astype(bf16)
    hid_near = (grad_near * near_slope).astype(bf16)

    far_pair = lax.all_gather(far_pair, "depth", axis=0, tiled=False)
    act_near = line_all_gather(act_near, 0, "col").reshape(n_col * bunch, near)
    act_near = lax.all_gather(act_near, "depth", axis=0, tiled=True)
    hid_near = line_all_gather(hid_near, 0, "col").reshape(n_col * bunch, near)
    act_near, hid_near = lax.optimization_barrier((act_near, hid_near))
    hid_near = lax.all_gather(hid_near, "depth", axis=0, tiled=True)
    far_pair = line_all_gather(far_pair, 1, "col").reshape(total, 2 * far)

    grad_down = jnp.concatenate(
        [outer(dy_cols, act_near), outer(dy_cols, far_pair[:, :far])], axis=1
    )
    grad_up = jnp.concatenate(
        [outer(x_cols, hid_near), outer(x_cols, far_pair[:, far:])], axis=1
    )

    def back(left, right):
        return lax.dot_general(
            left, right, (((1,), (1,)), ((), ())), preferred_element_type=f32
        )

    grad_in = back(hid_near, w_up[:, :near]) + back(far_pair[:, far:], w_up[:, near:])
    grad_in = grad_in.astype(bf16).reshape(group, rows, narrow)
    grad_in = lax.all_to_all(grad_in, ("depth", "row"), 0, 0, tiled=True)
    grad_in = grad_in.reshape(n_depth, n_row, rows, narrow).astype(f32).sum(axis=1)
    grad_in = jnp.transpose(grad_in, (1, 0, 2)).reshape(rows, part).astype(bf16)
    return (grad_in, grad_up, grad_down)


def solution(mesh):
    placed = (
        P(("depth", "row"), "col"),
        P(("depth", "row"), "col"),
        P(("col", "depth"), "row"),
        P(("col", "depth"), "row"),
    )
    return jax.shard_map(
        body,
        mesh=mesh,
        in_specs=placed,
        out_specs=(
            P(("depth", "row"), "col"),
            P(("col", "depth"), "row"),
            P(("col", "depth"), "row"),
        ),
        check_vma=False,
    )
```

```python
import math

import jax
import jax.numpy as jnp
from jax import lax
from jax.sharding import PartitionSpec as P


def gelu_parts(hidden):
    coeff = math.sqrt(2.0 / math.pi)
    cube = hidden * hidden * hidden
    slope_in = jnp.tanh(coeff * (hidden + 0.044715 * cube))
    value = 0.5 * hidden * (1.0 + slope_in)
    slope = 0.5 * (1.0 + slope_in) + 0.5 * hidden * (1.0 - slope_in * slope_in) * coeff * (
        1.0 + 3.0 * 0.044715 * hidden * hidden
    )
    return (value, slope)


def line_sums(parts, axis, name, steps, carry=None):
    count = lax.axis_size(name)
    here = lax.axis_index(name)

    def piece(index):
        return lax.dynamic_index_in_dim(
            parts, jnp.clip(index, 0, count - 1), axis, keepdims=False
        )

    for step in steps:
        send_up = piece(here + count - step)
        send_down = piece(here + step - count)
        if carry is not None:
            send_up, send_down = send_up + carry[0], send_down + carry[1]
        carry = (
            lax.ppermute(send_up, name, [(i, i + 1) for i in range(step)]),
            lax.ppermute(send_down, name, [(i, i - 1) for i in range(count - step, count)]),
        )
    return carry


def line_total(parts, axis, name, carry):
    own = lax.dynamic_index_in_dim(parts, lax.axis_index(name), axis, keepdims=False)
    up, down = carry
    return own.astype(jnp.float32) + up.astype(jnp.float32) + down.astype(jnp.float32)


def line_moves(block, name, steps, carry=None):
    count = lax.axis_size(name)
    ups, downs = carry if carry is not None else ([], [])
    for step in steps:
        up = ups[-1] if ups else block
        down = downs[-1] if downs else block
        ups = ups + [lax.ppermute(up, name, [(i, i + 1) for i in range(step - 1, count - 1)])]
        downs = downs + [lax.ppermute(down, name, [(i, i - 1) for i in range(1, count - step + 1)])]
    return ups, downs


def line_whole(block, axis, name, carry):
    count = lax.axis_size(name)
    here = lax.axis_index(name)
    ups, downs = carry
    shape = block.shape[:axis] + (count,) + block.shape[axis:]
    whole = lax.dynamic_update_index_in_dim(
        jnp.zeros(shape, block.dtype), block, here, axis
    )
    for step in range(1, count):
        arrived = jnp.where(here >= step, ups[step - 1], downs[count - step - 1])
        whole = lax.dynamic_update_index_in_dim(
            whole, arrived, lax.rem(here - step + count, count), axis
        )
    return whole


def body(tokens, grad_out, w_up, w_down):
    n_depth, n_row, n_col = (lax.axis_size(a) for a in ("depth", "row", "col"))
    rows, part = tokens.shape
    narrow, hidden = w_up.shape
    group = n_depth * n_row
    total = group * rows
    bunch = total // (n_depth * n_col)
    far = hidden // 4 // 128 * 128
    near = hidden - far
    bf16, f32 = jnp.bfloat16, jnp.float32

    both = jnp.stack([tokens, grad_out]).reshape(2, rows, n_depth, narrow)
    both = jnp.transpose(both, (2, 0, 1, 3))
    both = jnp.broadcast_to(both[:, None], (n_depth, n_row, 2, rows, narrow))
    both = both.reshape(group, 2, rows, narrow)
    both = lax.all_to_all(both, ("depth", "row"), 0, 0, tiled=True)
    x_cols = both[:, 0].reshape(total, narrow)
    dy_cols = both[:, 1].reshape(total, narrow)

    def product(left, right):
        return jnp.dot(left, right, preferred_element_type=f32).astype(bf16)

    def outer(left, right):
        return lax.dot_general(
            left, right, (((0,), (0,)), ((), ())), preferred_element_type=f32
        ).astype(bf16)

    steps = range(1, n_col)
    third = max(1, (n_col - 1) // 3)
    tie = lax.optimization_barrier

    pre_near = product(x_cols, w_up[:, :near])
    pre_near = lax.psum_scatter(pre_near, "depth", scatter_dimension=0, tiled=True)
    far_terms = jnp.concatenate(
        [product(x_cols, w_up[:, near:]), product(dy_cols, w_down[:, near:])], axis=1
    ).reshape(n_depth, n_col, bunch, 2 * far)
    far_move = line_sums(far_terms, 1, "col", steps[:-third])
    grad_near = product(dy_cols, w_down[:, :near])
    pre_near, grad_near, far_move = tie((pre_near, grad_near, far_move))

    grad_near = lax.psum_scatter(grad_near, "depth", scatter_dimension=0, tiled=True)
    far_move = line_sums(far_terms, 1, "col", steps[-third:], far_move)
    far_sum = line_total(far_terms, 1, "col", far_move).astype(bf16)
    pre_near = pre_near.reshape(n_col, bunch, near)
    pre_move = line_sums(pre_near, 0, "col", steps)
    grad_near, far_sum, pre_move = tie((grad_near, far_sum, pre_move))

    far_sum = lax.psum_scatter(
        far_sum.reshape(n_depth * bunch, 2 * far), "depth", scatter_dimension=0, tiled=True
    )
    grad_near = grad_near.reshape(n_col, bunch, near)
    grad_move = line_sums(grad_near, 0, "col", steps[:-third])
    far_sum, grad_move = tie((far_sum, grad_move))

    far_sum = far_sum.astype(f32)
    far_value, far_slope = gelu_parts(far_sum[:, :far])
    far_pair = jnp.concatenate(
        [far_value.astype(bf16), (far_sum[:, far:] * far_slope).astype(bf16)], axis=1
    )
    far_pair = lax.all_gather(far_pair, "depth", axis=0, tiled=False)
    grad_move = line_sums(grad_near, 0, "col", steps[-third:], grad_move)
    near_value, near_slope = gelu_parts(line_total(pre_near, 0, "col", pre_move))
    act_near = near_value.astype(bf16)
    hid_near = (line_total(grad_near, 0, "col", grad_move) * near_slope).astype(bf16)
    hid_move = line_moves(hid_near, "col", steps)
    far_pair, hid_near, hid_move = tie((far_pair, hid_near, hid_move))

    hid_near = line_whole(hid_near, 0, "col", hid_move).reshape(n_col * bunch, near)
    hid_near = lax.all_gather(hid_near, "depth", axis=0, tiled=True)
    act_move = line_moves(act_near, "col", steps)
    act_near = line_whole(act_near, 0, "col", act_move).reshape(n_col * bunch, near)
    far_move = line_moves(far_pair, "col", steps[:third])
    hid_near, act_near, far_move = tie((hid_near, act_near, far_move))

    act_near = lax.all_gather(act_near, "depth", axis=0, tiled=True)
    far_move = line_moves(far_pair, "col", steps[third:], far_move)
    far_pair = line_whole(far_pair, 1, "col", far_move).reshape(total, 2 * far)
    act_far, hid_far = far_pair[:, :far], far_pair[:, far:]

    def back(left, right):
        return lax.dot_general(
            left, right, (((1,), (1,)), ((), ())), preferred_element_type=f32
        )

    grad_in = back(hid_near, w_up[:, :near]) + back(hid_far, w_up[:, near:])
    grad_in = grad_in.astype(bf16).reshape(group, rows, narrow)
    grad_in = lax.all_to_all(grad_in, ("depth", "row"), 0, 0, tiled=True)
    grad_in = grad_in.reshape(n_depth, n_row, rows, narrow).astype(f32).sum(axis=1)
    grad_in = jnp.transpose(grad_in, (1, 0, 2)).reshape(rows, part).astype(bf16)
    grad_up = jnp.concatenate([outer(x_cols, hid_near), outer(x_cols, hid_far)], axis=1)
    down_far = outer(dy_cols, act_far)
    act_near, grad_in, grad_up, down_far = tie((act_near, grad_in, grad_up, down_far))
    grad_down = jnp.concatenate([outer(dy_cols, act_near), down_far], axis=1)
    return (grad_in, grad_up, grad_down)


def solution(mesh):
    placed = (
        P(("depth", "row"), "col"),
        P(("depth", "row"), "col"),
        P(("col", "depth"), "row"),
        P(("col", "depth"), "row"),
    )
    return jax.shard_map(
        body,
        mesh=mesh,
        in_specs=placed,
        out_specs=(
            P(("depth", "row"), "col"),
            P(("col", "depth"), "row"),
            P(("col", "depth"), "row"),
        ),
        check_vma=False,
    )
```

```python
import math

import jax
import jax.numpy as jnp
from jax import lax
from jax.sharding import PartitionSpec as P


def gelu_parts(hidden):
    coeff = math.sqrt(2.0 / math.pi)
    cube = hidden * hidden * hidden
    slope_in = jnp.tanh(coeff * (hidden + 0.044715 * cube))
    value = 0.5 * hidden * (1.0 + slope_in)
    slope = 0.5 * (1.0 + slope_in) + 0.5 * hidden * (1.0 - slope_in * slope_in) * coeff * (
        1.0 + 3.0 * 0.044715 * hidden * hidden
    )
    return (value, slope)


def line_sums(parts, axis, name, steps, carry=None):
    count = lax.axis_size(name)
    here = lax.axis_index(name)

    def piece(index):
        return lax.dynamic_index_in_dim(
            parts, jnp.clip(index, 0, count - 1), axis, keepdims=False
        )

    for step in steps:
        send_up = piece(here + count - step)
        send_down = piece(here + step - count)
        if carry is not None:
            send_up, send_down = send_up + carry[0], send_down + carry[1]
        carry = (
            lax.ppermute(send_up, name, [(i, i + 1) for i in range(step)]),
            lax.ppermute(send_down, name, [(i, i - 1) for i in range(count - step, count)]),
        )
    return carry


def line_total(parts, axis, name, carry):
    own = lax.dynamic_index_in_dim(parts, lax.axis_index(name), axis, keepdims=False)
    up, down = carry
    return own.astype(jnp.float32) + up.astype(jnp.float32) + down.astype(jnp.float32)


def line_moves(block, name, steps, carry=None):
    count = lax.axis_size(name)
    ups, downs = carry if carry is not None else ([], [])
    for step in steps:
        up = ups[-1] if ups else block
        down = downs[-1] if downs else block
        ups = ups + [lax.ppermute(up, name, [(i, i + 1) for i in range(step - 1, count - 1)])]
        downs = downs + [lax.ppermute(down, name, [(i, i - 1) for i in range(1, count - step + 1)])]
    return ups, downs


def line_whole(block, axis, name, carry):
    count = lax.axis_size(name)
    here = lax.axis_index(name)
    ups, downs = carry
    shape = block.shape[:axis] + (count,) + block.shape[axis:]
    whole = lax.dynamic_update_index_in_dim(
        jnp.zeros(shape, block.dtype), block, here, axis
    )
    for step in range(1, count):
        arrived = jnp.where(here >= step, ups[step - 1], downs[count - step - 1])
        whole = lax.dynamic_update_index_in_dim(
            whole, arrived, lax.rem(here - step + count, count), axis
        )
    return whole


def body(tokens, grad_out, w_up, w_down):
    n_depth, n_row, n_col = (lax.axis_size(a) for a in ("depth", "row", "col"))
    rows, part = tokens.shape
    narrow, hidden = w_up.shape
    group = n_depth * n_row
    total = group * rows
    bunch = total // (n_depth * n_col)
    far = hidden // 4 // 128 * 128
    near = hidden - far
    bf16, f32 = jnp.bfloat16, jnp.float32

    both = jnp.stack([tokens, grad_out]).reshape(2, rows, n_depth, narrow)
    both = jnp.transpose(both, (2, 0, 1, 3))
    both = jnp.broadcast_to(both[:, None], (n_depth, n_row, 2, rows, narrow))
    both = both.reshape(group, 2, rows, narrow)
    both = lax.all_to_all(both, ("depth", "row"), 0, 0, tiled=True)
    x_cols = both[:, 0].reshape(total, narrow)
    dy_cols = both[:, 1].reshape(total, narrow)

    def product(left, right):
        return jnp.dot(left, right, preferred_element_type=f32).astype(bf16)

    def outer(left, right):
        return lax.dot_general(
            left, right, (((0,), (0,)), ((), ())), preferred_element_type=f32
        ).astype(bf16)

    steps = range(1, n_col)
    third = max(1, (n_col - 1) // 3)
    tie = lax.optimization_barrier

    pre_near = product(x_cols, w_up[:, :near])
    pre_near = lax.psum_scatter(pre_near, "depth", scatter_dimension=0, tiled=True)
    far_terms = jnp.concatenate(
        [product(x_cols, w_up[:, near:]), product(dy_cols, w_down[:, near:])], axis=1
    ).reshape(n_depth, n_col, bunch, 2 * far)
    far_move = line_sums(far_terms, 1, "col", steps[:-third])
    grad_near = product(dy_cols, w_down[:, :near])
    pre_near, grad_near, far_move = tie((pre_near, grad_near, far_move))

    grad_near = lax.psum_scatter(grad_near, "depth", scatter_dimension=0, tiled=True)
    far_move = line_sums(far_terms, 1, "col", steps[-third:], far_move)
    far_sum = line_total(far_terms, 1, "col", far_move).astype(bf16)
    pre_near = pre_near.reshape(n_col, bunch, near)
    pre_move = line_sums(pre_near, 0, "col", steps)
    grad_near, far_sum, pre_move = tie((grad_near, far_sum, pre_move))

    near_value, near_slope = gelu_parts(line_total(pre_near, 0, "col", pre_move))
    act_near = near_value.astype(bf16)
    far_sum = lax.psum_scatter(
        far_sum.reshape(n_depth * bunch, 2 * far), "depth", scatter_dimension=0, tiled=True
    )
    act_move = line_moves(act_near, "col", steps[:-third])
    far_sum, act_move = tie((far_sum, act_move))

    far_sum = far_sum.astype(f32)
    far_value, far_slope = gelu_parts(far_sum[:, :far])
    far_pair = jnp.concatenate(
        [far_value.astype(bf16), (far_sum[:, far:] * far_slope).astype(bf16)], axis=1
    )
    far_pair = lax.all_gather(far_pair, "depth", axis=0, tiled=False)
    act_move = line_moves(act_near, "col", steps[-third:], act_move)
    act_near = line_whole(act_near, 0, "col", act_move).reshape(n_col * bunch, near)
    grad_near = grad_near.reshape(n_col, bunch, near)
    grad_move = line_sums(grad_near, 0, "col", steps[:third])
    far_pair, act_near, grad_move = tie((far_pair, act_near, grad_move))

    act_near = lax.all_gather(act_near, "depth", axis=0, tiled=True)
    grad_move = line_sums(grad_near, 0, "col", steps[third:], grad_move)
    hid_near = (line_total(grad_near, 0, "col", grad_move) * near_slope).astype(bf16)
    hid_move = line_moves(hid_near, "col", steps)
    hid_near = line_whole(hid_near, 0, "col", hid_move).reshape(n_col * bunch, near)
    far_move = line_moves(far_pair, "col", steps[:third])
    act_near, hid_near, far_move = tie((act_near, hid_near, far_move))

    hid_near = lax.all_gather(hid_near, "depth", axis=0, tiled=True)
    far_move = line_moves(far_pair, "col", steps[third:], far_move)
    far_pair = line_whole(far_pair, 1, "col", far_move).reshape(total, 2 * far)
    act_far, hid_far = far_pair[:, :far], far_pair[:, far:]

    def back(left, right):
        return lax.dot_general(
            left, right, (((1,), (1,)), ((), ())), preferred_element_type=f32
        )

    grad_down = jnp.concatenate([outer(dy_cols, act_near), outer(dy_cols, act_far)], axis=1)
    up_far = outer(x_cols, hid_far)
    in_far = back(hid_far, w_up[:, near:])
    hid_near, grad_down, up_far, in_far = tie((hid_near, grad_down, up_far, in_far))

    grad_in = (back(hid_near, w_up[:, :near]) + in_far).astype(bf16)
    grad_in, hid_near = tie((grad_in, hid_near))
    grad_in = grad_in.reshape(group, rows, narrow)
    grad_in = lax.all_to_all(grad_in, ("depth", "row"), 0, 0, tiled=True)
    grad_in = grad_in.reshape(n_depth, n_row, rows, narrow).astype(f32).sum(axis=1)
    grad_in = jnp.transpose(grad_in, (1, 0, 2)).reshape(rows, part).astype(bf16)
    grad_up = jnp.concatenate([outer(x_cols, hid_near), up_far], axis=1)
    return (grad_in, grad_up, grad_down)


def solution(mesh):
    placed = (
        P(("depth", "row"), "col"),
        P(("depth", "row"), "col"),
        P(("col", "depth"), "row"),
        P(("col", "depth"), "row"),
    )
    return jax.shard_map(
        body,
        mesh=mesh,
        in_specs=placed,
        out_specs=(
            P(("depth", "row"), "col"),
            P(("col", "depth"), "row"),
            P(("col", "depth"), "row"),
        ),
        check_vma=False,
    )
```
